32 devices in a mesh: mode: 8 (over z, x), slab: 4 (over y, core).
Axes of the slice: x: 2, y: 2, z: 4, core: 2. Of those that a mesh axis runs over, the one named last changes fastest.
Arguments:
- field: float32 [128, 16, 64, 128], P('mode', 'slab'), may hold values from -6 to 6
- coefficient_fields: float32 [16, 16, 64, 128], P(None, 'slab', 'mode'), may hold values from -6 to 6
- triple_blocks: float32 [16, 4, 32, 64], replicated, may hold values from -0.1875 to 0.1875
- block_pattern: int32 [16, 4, 2], replicated, may hold values from 0 to 3
Outputs:
- result: float32 [128, 16, 64, 128], P('mode', 'slab')
The draws below stay inside these ranges and needn't reach their ends.
All inputs are finite; a program needn't handle non-finite values.
Results may differ from the reference program's by a relative error of at most 0.0003.
Values sent between devices are 32-bit elements; how exact they have to be, the bound alone decides.
No kernel may reach another device: no remote copies, remote signals or barrier semaphores. Data moves between devices by JAX's collectives and lax.ppermute only.
A program may use at most 128 MiB of HBM per device.

```python
import jax
import jax.numpy as jnp
from jax import lax

P_SIZE = 128
MB = 32
PB = 4
NNZ = 2
K = 16
NX = 128
NY = 64
NZ = 16


def touch_ends(result, rng, least, top_value):
    longest = result.shape.index(max(result.shape))
    spots = []
    for shift in (0, 1):
        where = [jax.random.randint(jax.random.fold_in(rng, axis), (), 0, length) for axis, length in enumerate(result.shape)]
        where[longest] = (where[longest] + shift) % result.shape[longest]
        spots.append(tuple(where))
    return result.at[spots[0]].set(least).at[spots[1]].set(top_value)


def shard_levels(own_key, extent, shards, least, top_value):
    loudness = 1.0
    for position, blocks in shards:
        heights = jax.random.uniform(jax.random.fold_in(jax.random.fold_in(own_key, 6), position), (blocks,), jnp.float32, least / len(shards), top_value / len(shards))
        loudness = loudness * jnp.repeat(jnp.exp(heights), extent[position] // blocks).reshape((-1,) + (1,) * (len(extent) - 1 - position))
    return loudness


def normal_values(own_key, extent, width, most, cuts=(), kind=jnp.bfloat16):
    gain = shard_levels(own_key, extent, cuts, -0.22, 0.18) if cuts else 1.0
    values = jax.random.normal(own_key, extent, jnp.float32) * width * gain
    return jnp.minimum(jnp.maximum(values, -most), most).astype(kind)


def setup_inputs(seed: int = 0) -> dict:
    seeds = jax.random.split(jax.random.key(seed), 5)
    return {
        "field": normal_values(seeds[0], (P_SIZE, NZ, NY, NX), 1.0, 6.0, ((0, 8), (1, 4)), jnp.float32),
        "coefficient_fields": normal_values(seeds[1], (K, NZ, NY, NX), 1.0, 6.0, ((1, 4), (2, 8)), jnp.float32),
        "triple_blocks": normal_values(seeds[2], (K, PB, MB, NNZ * MB), (K * NNZ * MB) ** -0.5, 0.1875, (), jnp.float32),
        "block_pattern": touch_ends(jax.random.randint(seeds[3], (K, PB, NNZ), 0, PB), jax.random.fold_in(seeds[3], 1), 0, PB - 1).astype(jnp.int32),
    }


def gradients(centre, ahead):
    zero_x = jnp.zeros_like(centre[..., :1])
    grad_x = jnp.concatenate([centre[..., 1:], zero_x], axis=-1) - centre
    zero_y = jnp.zeros_like(centre[:, :1])
    grad_y = jnp.concatenate([centre[:, 1:], zero_y], axis=1) - centre
    grad_z = ahead - centre
    return jnp.stack([grad_x, grad_y, grad_z])


def couple(gradient, weights_here, triple_blocks, block_pattern):
    count = gradient.shape[-1]
    blocked = gradient.reshape(3, PB, MB, count)

    def add_term(index, total):
        selected = jnp.take(blocked, block_pattern[index], axis=1).reshape(3, PB, NNZ * MB, count)
        product = jnp.einsum("rij,drjn->drin", triple_blocks[index], selected, precision=lax.Precision.HIGHEST)
        return total + product * weights_here[index]

    total = lax.fori_loop(0, K, add_term, jnp.zeros((3, PB, MB, count), jnp.float32))
    return total.reshape(3, PB * MB, count)


def reference(field, coefficient_fields, triple_blocks, block_pattern):
    zeros_plane = jnp.zeros((P_SIZE, NY, NX), jnp.float32)

    def plane_step(lower_flux, depth):
        centre = lax.dynamic_index_in_dim(field, depth, 1, keepdims=False)
        ahead = lax.dynamic_index_in_dim(field, jnp.minimum(depth + 1, NZ - 1), 1, keepdims=False)
        ahead = jnp.where(depth + 1 < NZ, ahead, zeros_plane)
        gradient = gradients(centre, ahead).reshape(3, P_SIZE, NY * NX)
        weights_here = lax.dynamic_index_in_dim(coefficient_fields, depth, 1, keepdims=False).reshape(K, NY * NX)
        flux = couple(gradient, weights_here, triple_blocks, block_pattern).reshape(3, P_SIZE, NY, NX)
        flux_x, flux_y, flux_z = flux[0], flux[1], flux[2]
        part_x = jnp.concatenate([jnp.zeros_like(flux_x[..., :1]), flux_x[..., :-1]], axis=-1) - flux_x
        part_y = jnp.concatenate([jnp.zeros_like(flux_y[:, :1]), flux_y[:, :-1]], axis=1) - flux_y
        result_plane = part_x + part_y + (lower_flux - flux_z)
        return flux_z, result_plane

    final_flux, planes = lax.scan(plane_step, zeros_plane, jnp.arange(NZ, dtype=jnp.int32))
    return jnp.transpose(planes, (1, 0, 2, 3))
```

```python
import functools

import jax
import jax.numpy as jnp
from jax import lax
from jax.experimental import pallas as pl
from jax.experimental.pallas import tpu as pltpu
from jax.sharding import PartitionSpec as P

F32 = jnp.float32
BF16 = jnp.bfloat16
VMEM = pl.BlockSpec(memory_space=pltpu.VMEM)
SMEM = pl.BlockSpec(memory_space=pltpu.SMEM)
MIB = 2**20


def params(mib):
    return pltpu.CompilerParams(vmem_limit_bytes=mib * MIB)


def cost(flops, size):
    return pl.CostEstimate(flops=int(flops), bytes_accessed=int(size), transcendentals=0)


def from_behind(value, axis, steps):
    count = lax.axis_size(axis)
    first, last = (max(0, -steps), min(count, count - steps))
    return lax.ppermute(value, axis, [(source, source + steps) for source in range(first, last)])


def swap_pieces(pieces):
    count = len(pieces)
    half = count // 2
    order = [s for pair in zip(range(half, count), [0] + list(range(1, half))) for s in pair if s]
    received = list(pieces)
    for s in order:
        received[s] = lax.ppermute(pieces[s], "mode", [(i, i ^ s) for i in range(count)])
    return received


def exchange(pieces):
    if len(pieces) == 1:
        return [lax.all_to_all(pieces[0], "mode", split_axis=0, concat_axis=0, tiled=True)]
    return swap_pieces(pieces)


def each_piece(me, refs):
    if len(refs) == 1:
        return [(owner, refs[0].at[owner]) for owner in range(refs[0].shape[0])]
    return [(me ^ s, ref) for s, ref in enumerate(refs)]


def part_of(owner, size):
    return pl.ds(owner * size if isinstance(owner, int) else pl.multiple_of(owner * size, size), size)


def pieces_shape(count, whole, shape):
    if whole:
        return [jax.ShapeDtypeStruct((count,) + shape, F32)]
    return [jax.ShapeDtypeStruct(shape, F32)] * count


def pieces_specs(shapes, first, planes):
    specs = []
    for array in shapes:
        lead = array.shape[:-4]
        zeros = (0,) * len(lead)
        block = lead + (1,) + array.shape[-3:]
        specs.append(pl.BlockSpec(block, lambda i, zeros=zeros: zeros + (jnp.clip(i - first, 0, planes - 1), 0, 0, 0)))
    return specs


def split(value):
    high = value.astype(BF16)
    return high, (value - high.astype(F32)).astype(BF16)


def prepare_kernel(pattern_ref, blocks_ref, field_ref, dense_ref, weights_ref):
    fields, row_blocks, block, stored = blocks_ref.shape
    modes = row_blocks * block
    lane = lax.broadcasted_iota(jnp.int32, (block, modes), 1)

    def one_field(k, carry):
        for r in range(row_blocks):
            value = blocks_ref[k, r]
            value = jnp.concatenate([value, jnp.zeros((block, modes - stored), F32)], axis=1)
            total = None
            for c in range(stored // block):
                part = jnp.where((lane >= c * block) & (lane < (c + 1) * block), value, 0.0)
                shift = lax.rem(pattern_ref[k, r, c] - c + row_blocks, row_blocks) * block
                part = pltpu.roll(part, shift, 1)
                total = part if total is None else total + part
            high, low = split(total)
            rows = pl.ds(pl.multiple_of(k * modes + r * block, block), block)
            dense_ref[rows, 0:modes] = high
            dense_ref[rows, modes : 2 * modes] = low
            dense_ref[rows, 2 * modes :] = high
        return carry

    lax.fori_loop(0, fields, one_field, 0)
    for z in range(weights_ref.shape[0]):
        weights_ref[z] = jnp.swapaxes(field_ref[:, z], 0, 1)


def prepare(triple_blocks, block_pattern, coefficient_fields):
    fields, row_blocks, block, _ = triple_blocks.shape
    modes = row_blocks * block
    _, depth, rows, width = coefficient_fields.shape
    return pl.pallas_call(
        prepare_kernel,
        in_specs=[SMEM, VMEM, VMEM],
        out_specs=[VMEM, VMEM],
        out_shape=[
            jax.ShapeDtypeStruct((fields * modes, 3 * modes), BF16),
            jax.ShapeDtypeStruct((depth, rows, fields, width), F32),
        ],
        compiler_params=params(16),
        cost_estimate=cost(3e9, 4 * MIB),
        name="prepare",
    )(block_pattern, triple_blocks, coefficient_fields)


def pack_kernel(count, chunks, me_ref, field_ref, *refs):
    me = me_ref[0]
    step = pl.program_id(0)
    rows = field_ref.shape[2] // count
    refs = list(refs)
    first = 0
    for planes, number in chunks:

        @pl.when((step >= first) & (step < first + planes))
        def _(outs=[refs.pop(0) for _ in range(number)]):
            for owner, out in each_piece(me, outs):
                own = field_ref[:, 0, part_of(owner, rows), :]
                out[0, :rows] = jnp.swapaxes(own, 0, 1)
                ahead = field_ref[:, 0, part_of(after(owner, count), rows), :][:, 0]
                out[0, rows] = jnp.where(owner < count - 1, ahead, 0.0)

        first += planes


def after(owner, count):
    return min(owner + 1, count - 1) if isinstance(owner, int) else jnp.minimum(owner + 1, count - 1)


def pack(me, field, chunks, count):
    modes, _, height, width = field.shape
    rows = height // count
    order = [plane for planes, _ in chunks for plane in planes]

    def plane_of(i):
        value = order[-1]
        for j, plane in enumerate(order[:-1]):
            value = jnp.where(i == j, plane, value)
        return (0, value, 0, 0)

    out_specs, out_shape, plan, first = [], [], [], 0
    for planes, whole in chunks:
        shapes = pieces_shape(count, whole, (len(planes), rows + 1, modes, width))
        out_specs += pieces_specs(shapes, first, len(planes))
        out_shape += shapes
        plan.append((len(planes), len(shapes)))
        first += len(planes)
    pieces = pl.pallas_call(
        functools.partial(pack_kernel, count, plan),
        grid=(len(order),),
        in_specs=[SMEM, pl.BlockSpec((modes, 1, height, width), plane_of)],
        out_specs=out_specs,
        out_shape=out_shape,
        compiler_params=params(16),
        cost_estimate=cost(0, 8 * len(order) * modes * height * width),
        name="pack",
    )(me, field)
    pieces = list(pieces)
    return [[pieces.pop(0) for _ in range(number)] for _, number in plan]


def edges_kernel(number, picks, me_ref, *refs):
    me = me_ref[0]
    ins, outs = refs[:number], refs[number:]
    rows = outs[0].shape[0]
    for out, index in zip(outs, picks):
        for owner, ref in each_piece(me, ins):
            out[:, part_of(owner, ref.shape[-2]), :] = ref[index, :rows]


def edges(me, received, picks, count):
    rows, size, width = received[0].shape[-3:]
    shape = jax.ShapeDtypeStruct((rows - 1, size * count, width), F32)
    return pl.pallas_call(
        functools.partial(edges_kernel, len(received), picks),
        in_specs=[SMEM] + [VMEM] * len(received),
        out_specs=[VMEM] * len(picks),
        out_shape=[shape] * len(picks),
        compiler_params=params(16),
        cost_estimate=cost(0, 16 * rows * size * count * width),
        name="edges",
    )(me, *received)


def ahead_x(value):
    width = value.shape[-1]
    lane = lax.broadcasted_iota(jnp.int32, value.shape, 1)
    return jnp.where(lane == width - 1, 0.0, pltpu.roll(value, width - 1, 1))


def behind_x(value):
    lane = lax.broadcasted_iota(jnp.int32, value.shape, 1)
    return jnp.where(lane == 0, 0.0, pltpu.roll(value, 1, 1))


def couple(c_ref, rhs_ref, groups, weights, per_step):
    flat = [gradient for group in groups for gradient in group]
    owner = [r for r, group in enumerate(groups) for _ in group]
    modes, width = flat[0].shape
    for i, gradient in enumerate(flat):
        high, low = split(gradient)
        lanes = slice(i * width, (i + 1) * width)
        rhs_ref[0:modes, lanes] = high
        rhs_ref[modes : 2 * modes, lanes] = high
        rhs_ref[2 * modes :, lanes] = low
    rhs = rhs_ref[:, : len(flat) * width]
    fields = c_ref.shape[0] // modes
    totals = [None] * len(flat)
    for k0 in range(0, fields, per_step):
        product = jnp.dot(c_ref[k0 * modes : (k0 + per_step) * modes, :], rhs, preferred_element_type=F32)
        for k in range(per_step):
            for i in range(len(flat)):
                part = product[k * modes : (k + 1) * modes, i * width : (i + 1) * width]
                part = part * weights[owner[i]][k0 + k : k0 + k + 1, :]
                totals[i] = part if totals[i] is None else totals[i] + part
    return totals


def flux_kernel(plan, me_ref, c_ref, *refs):
    tasks, sources, weights, sums_in, final, number_out, carried = plan
    me = me_ref[0]
    refs = list(refs)
    weight_refs = [refs.pop(0) for _ in range(1 + max(array for array, _ in weights.values()))]
    ins = {plane: [refs.pop(0) for _ in range(number)] for plane, (number, _) in sources.items()}
    sums = {plane: [refs.pop(0) for _ in range(number)] for plane, number in sums_in.items()}
    outs = [refs.pop(0) for _ in range(number_out)]
    goes_on = {plane: refs.pop(0) for plane in carried}
    planes_ref, rhs_ref = refs.pop(0), refs.pop(0)
    total = dict(goes_on)
    for plane in final:
        total[plane] = refs.pop(0)
    _, full_rows, modes, width = planes_ref.shape
    rows = full_rows - 1
    slot = {}
    for plane, group in ins.items():
        slot[plane] = len(slot)
        if len(group[0].shape) == 3:
            planes_ref[slot[plane], :rows] = group[0][...]
        else:
            for owner, ref in each_piece(me, group):
                planes_ref[slot[plane], :, part_of(owner, ref.shape[-2]), :] = ref[sources[plane][1]]
    for plane, ref in total.items():
        if plane in sums:
            ref[...] = functools.reduce(lambda left, right: left + right, [array[...] for array in sums[plane]])
        else:
            ref[...] = jnp.zeros_like(ref)

    def weight(plane, y):
        array, index = weights[plane]
        return weight_refs[array][index, y]

    for plane, directions in tasks:
        per_step = 2

        def step(i, carry, plane=plane, directions=directions):
            groups = []
            for j in range(per_step):
                y = per_step * i + j
                here = planes_ref[slot[plane], y]
                group = []
                if "x" in directions:
                    group.append(ahead_x(here) - here)
                if "y" in directions:
                    group.append(planes_ref[slot[plane], y + 1] - here)
                if "z" in directions:
                    group.append(planes_ref[slot[plane + 1], y] - here)
                groups.append(group)
            fluxes = couple(c_ref, rhs_ref, groups, [weight(plane, per_step * i + j) for j in range(per_step)], 4)
            here = total.get(plane)
            after = total.get(plane + 1)
            for j in range(per_step):
                y = per_step * i + j
                change = None
                for direction in directions:
                    flux = fluxes.pop(0)
                    part = behind_x(flux) - flux if direction == "x" else -flux
                    change = part if change is None else change + part
                    if direction == "y":
                        here[y + 1] += flux
                    if direction == "z" and after is not None:
                        after[y] += flux
                if here is not None:
                    here[y] += change
            return carry

        lax.fori_loop(0, rows // per_step, step, 0)
    for owner, out in each_piece(me, outs):
        for z, plane in enumerate(final):
            out[z] = total[plane][:, part_of(owner, out.shape[-2]), :]


def fluxes(me, dense, weight_arrays, tasks, sources, weights, sums, final, whole, carried, count):
    rows, fields, width = weight_arrays[0].shape[1:]
    modes = dense.shape[1] // 3
    size = modes // count
    out_shape = pieces_shape(count, whole, (len(final), rows + 1, size, width)) if final else []
    number_out = len(out_shape)
    numbers = {p: len(a) for p, a in sums.items()}
    plan = (tasks, {p: (len(a), i) for p, (a, i) in sources.items()}, weights, numbers, final, number_out, carried)
    args = list(weight_arrays) + [array for arrays, _ in sources.values() for array in arrays]
    args += [array for arrays in sums.values() for array in arrays]
    plane_sum = (rows + 1, modes, width)
    out_shape = out_shape + [jax.ShapeDtypeStruct(plane_sum, F32)] * len(carried)
    widest = max(len(directions) for _, directions in tasks)
    scratch = [pltpu.VMEM((len(sources),) + plane_sum, F32), pltpu.VMEM((3 * modes, 2 * widest * width), BF16)]
    scratch += [pltpu.VMEM(plane_sum, F32)] * len(final)
    units = rows * sum(len(directions) for _, directions in tasks)
    results = pl.pallas_call(
        functools.partial(flux_kernel, plan),
        in_specs=[SMEM, VMEM] + [VMEM] * len(args),
        out_specs=[VMEM] * len(out_shape),
        out_shape=out_shape,
        scratch_shapes=scratch,
        compiler_params=params(32),
        cost_estimate=cost(units * 2 * dense.shape[0] * 4 * modes * width, 8 * MIB),
        name="fluxes_" + "_".join(f"{plane}{directions}" for plane, directions in tasks),
    )(me, dense, *args)
    return results[:number_out], dict(zip(carried, results[number_out:]))


def unpack_kernel(count, chunks, me_ref, *refs):
    me = me_ref[0]
    step = pl.program_id(0)
    refs = list(refs)
    out = refs.pop()
    first = 0
    for planes, number in chunks:

        @pl.when((step >= first) & (step < first + planes))
        def _(ins=[refs.pop(0) for _ in range(number)]):
            for owner, ref in each_piece(me, ins):
                rows = ref.shape[-3] - 1
                out[:, 0, part_of(owner, rows), :] = jnp.swapaxes(ref[0, :rows], 0, 1)
            for owner, ref in each_piece(me, ins):
                there = part_of(after(owner, count), rows)
                added = jnp.where(owner < count - 1, ref[0, rows], 0.0)[:, None, :]
                value = out[:, 0, there, :]
                row = lax.broadcasted_iota(jnp.int32, value.shape, 1)
                out[:, 0, there, :] = value + jnp.where(row == 0, added, 0.0)

        first += planes


def unpack(me, received, chunks, shape, count):
    modes, depth, height, width = shape
    in_specs, args, plan, first = [SMEM], [me], [], 0
    for planes, pieces in zip(chunks, received):
        in_specs += pieces_specs(pieces, first, len(planes))
        args += list(pieces)
        plan.append((len(planes), len(pieces)))
        first += len(planes)
    return pl.pallas_call(
        functools.partial(unpack_kernel, count, plan),
        grid=(depth,),
        in_specs=in_specs,
        out_specs=pl.BlockSpec((modes, 1, height, width), lambda i: (0, i, 0, 0)),
        out_shape=jax.ShapeDtypeStruct(shape, F32),
        compiler_params=params(16),
        cost_estimate=cost(0, 8 * depth * modes * height * width),
        name="unpack",
    )(*args)


WHOLE = (False, True, False, True)


def body(field, coefficient_fields, triple_blocks, block_pattern):
    count = lax.axis_size("mode")
    depth = field.shape[1]
    top = depth - 1
    me = lax.axis_index("mode").astype(jnp.int32).reshape(1)

    outer, inner = (top, 0), tuple(range(1, top))
    sent_outer, sent_inner = pack(me, field, ((outer, WHOLE[0]), (inner, WHOLE[1])), count)
    sent_outer = exchange(sent_outer)
    dense, weights = prepare(triple_blocks, block_pattern, coefficient_fields)
    sent_inner = exchange(sent_inner)
    (lowest,) = edges(me, sent_outer, (1,), count)
    above = from_behind(lowest, "slab", -1)

    arrays = {0: (sent_outer, 1), top: (sent_outer, 0), depth: ([above], 0)}
    for i, plane in enumerate(inner):
        arrays[plane] = (sent_inner, i)

    def add(tasks, sums, final, whole, carried):
        needed = sorted({p for p, _ in tasks} | {p + 1 for p, directions in tasks if "z" in directions})
        where = {p: (0, p) for p, _ in tasks}
        return fluxes(me, dense, [weights], tasks, {p: arrays[p] for p in needed}, where, sums, final, whole, carried, count)

    half = depth // 2
    _, early = add(((0, "xy"), (top, "xy")), {}, (), False, (0, top))
    _, last = add(((top, "z"),), {top: [early[top]]}, (), False, (top, depth))
    below = from_behind(last[depth], "slab", 1)
    tasks = ((0, "z"),) + tuple((p, "xyz") for p in range(1, half))
    pieces, carry = add(tasks, {0: [early[0], below]}, tuple(range(half)), WHOLE[2], (half,))
    back_first = exchange(pieces)
    tasks = tuple((p, "xyz") for p in range(half, top))
    pieces, _ = add(tasks, {half: [carry[half]], top: [last[top]]}, tuple(range(half, depth)), WHOLE[3], ())
    back_second = exchange(pieces)
    chunks = (tuple(range(half)), tuple(range(half, depth)))
    return unpack(me, (back_first, back_second), chunks, field.shape, count)


def solution(mesh):
    in_specs = (P("mode", "slab", None, None), P(None, "slab", "mode", None), P(), P())
    out_specs = P("mode", "slab", None, None)
    return jax.shard_map(body, mesh=mesh, in_specs=in_specs, out_specs=out_specs, check_vma=False)
```

```python
import functools

import jax
import jax.numpy as jnp
from jax import lax
from jax.experimental import pallas as pl
from jax.experimental.pallas import tpu as pltpu
from jax.sharding import PartitionSpec as P

F32 = jnp.float32
BF16 = jnp.bfloat16
VMEM = pl.BlockSpec(memory_space=pltpu.VMEM)
SMEM = pl.BlockSpec(memory_space=pltpu.SMEM)
MIB = 2**20


def params(mib):
    return pltpu.CompilerParams(vmem_limit_bytes=mib * MIB)


def cost(flops, size):
    return pl.CostEstimate(flops=int(flops), bytes_accessed=int(size), transcendentals=0)


def from_behind(value, axis, steps):
    count = lax.axis_size(axis)
    first, last = (max(0, -steps), min(count, count - steps))
    return lax.ppermute(value, axis, [(source, source + steps) for source in range(first, last)])


def exchange(pieces, order):
    count = len(pieces)
    received = list(pieces)
    for s in order:
        received[s] = lax.ppermute(pieces[s], "mode", [(i, i ^ s) for i in range(count)])
    return received


def part_of(owner, size):
    return pl.ds(pl.multiple_of(owner * size, size), size)


def after(owner, count):
    return jnp.minimum(owner + 1, count - 1)


def split(value):
    high = value.astype(BF16)
    return high, (value - high.astype(F32)).astype(BF16)


def prepare_kernel(count, me_ref, pattern_ref, blocks_ref, field_ref, *outs):
    dense_refs, weights_ref = outs[:4], outs[4]
    fields, row_blocks, block, stored = blocks_ref.shape
    modes = row_blocks * block
    half = modes // 2
    lane = lax.broadcasted_iota(jnp.int32, (block, modes), 1)
    side = me_ref[0] // (count // 2)

    def one_field(k, carry):
        for j in range(row_blocks):
            rows_side, local = divmod(j, row_blocks // 2)
            r = (side ^ rows_side) * (row_blocks // 2) + local
            value = blocks_ref[k, r]
            value = jnp.concatenate([value, jnp.zeros((block, modes - stored), F32)], axis=1)
            total = None
            for c in range(stored // block):
                part = jnp.where((lane >= c * block) & (lane < (c + 1) * block), value, 0.0)
                shift = lax.rem(pattern_ref[k, r, c] - c + row_blocks, row_blocks) * block
                part = pltpu.roll(part, shift, 1)
                total = part if total is None else total + part
            total = pltpu.roll(total, side * half, 1)
            high, low = (part.astype(F32) for part in split(total))
            other_high, other_low = pltpu.roll(high, half, 1), pltpu.roll(low, half, 1)
            rows = pl.ds(pl.multiple_of(k * half + local * block, block), block)
            near = jnp.where(lane < half, high, other_low).astype(BF16), high[:, :half].astype(BF16)
            far = jnp.where(lane < half, other_high, low).astype(BF16), other_high[:, :half].astype(BF16)
            for columns_side, parts in enumerate((near, far)):
                dense_refs[2 * columns_side + rows_side][rows, 0:modes] = parts[0]
                dense_refs[2 * columns_side + rows_side][rows, modes:] = parts[1]
        return carry

    lax.fori_loop(0, fields, one_field, 0)
    for z in range(weights_ref.shape[0]):
        weights_ref[z] = jnp.swapaxes(field_ref[:, z], 0, 1)


def prepare(me, triple_blocks, block_pattern, coefficient_fields, count):
    fields, row_blocks, block, _ = triple_blocks.shape
    modes = row_blocks * block
    _, depth, rows, width = coefficient_fields.shape
    part = jax.ShapeDtypeStruct((fields * modes // 2, 3 * modes // 2), BF16)
    *parts, weights = pl.pallas_call(
        functools.partial(prepare_kernel, count),
        in_specs=[SMEM, SMEM, VMEM, VMEM],
        out_specs=[VMEM] * 5,
        out_shape=[part] * 4 + [jax.ShapeDtypeStruct((depth, rows, fields, width), F32)],
        compiler_params=params(16),
        cost_estimate=cost(1, 1),
        name="prepare",
    )(me, block_pattern, triple_blocks, coefficient_fields)
    return {(i // 2, i % 2): part for i, part in enumerate(parts)}, weights


def pack_kernel(count, me_ref, field_ref, *outs):
    me = me_ref[0]
    rows = field_ref.shape[2] // count
    for s, out in enumerate(outs):
        owner = me ^ s
        own = field_ref[:, 0, part_of(owner, rows), :]
        out[0, :rows] = jnp.swapaxes(own, 0, 1)
        ahead = field_ref[:, 0, part_of(after(owner, count), rows), :][:, 0]
        out[0, rows] = jnp.where(owner < count - 1, ahead, 0.0)


def pack(me, field, count):
    modes, depth, height, width = field.shape
    rows = height // count
    block = (1, rows + 1, modes, width)
    return pl.pallas_call(
        functools.partial(pack_kernel, count),
        grid=(depth,),
        in_specs=[SMEM, pl.BlockSpec((modes, 1, height, width), lambda i: (0, i, 0, 0))],
        out_specs=[pl.BlockSpec(block, lambda i: (i, 0, 0, 0))] * count,
        out_shape=[jax.ShapeDtypeStruct((depth,) + block[1:], F32)] * count,
        compiler_params=params(16),
        cost_estimate=cost(1, 1),
        name="pack",
    )(me, field)


def half_row(me, s, count, size):
    return part_of((me ^ s) & (count // 2 - 1), size)


def ahead_x(value):
    width = value.shape[-1]
    lane = lax.broadcasted_iota(jnp.int32, value.shape, 1)
    return jnp.where(lane == width - 1, 0.0, pltpu.roll(value, width - 1, 1))


def behind_x(value):
    lane = lax.broadcasted_iota(jnp.int32, value.shape, 1)
    return jnp.where(lane == 0, 0.0, pltpu.roll(value, 1, 1))


def edges_kernel(count, picks, me_ref, *refs):
    me = me_ref[0]
    near, far, outs = refs[: len(picks)], refs[len(picks) : len(picks) + count // 2], refs[len(picks) + count // 2 :]
    for out, own, index in zip(outs, near, picks):
        rows, modes, _ = out.shape
        out[:, : modes // 2, :] = own[...]
        for i, ref in enumerate(far):
            size = ref.shape[2]
            start = modes // 2 + ((me ^ (i + count // 2)) & (count // 2 - 1)) * size
            out[:, pl.ds(pl.multiple_of(start, size), size), :] = ref[index, :rows]


def edges(me, near, far, picks, count):
    rows, half, width = near[0].shape
    return pl.pallas_call(
        functools.partial(edges_kernel, count, picks),
        in_specs=[SMEM] + [VMEM] * (len(near) + len(far)),
        out_specs=[VMEM] * len(picks),
        out_shape=[jax.ShapeDtypeStruct((rows, 2 * half, width), F32)] * len(picks),
        compiler_params=params(16),
        cost_estimate=cost(1, 1),
        name="edges",
    )(me, *near, *far)


def couple(c_refs, rhs_ref, groups, weights, per_step):
    flat = [gradient for group in groups for gradient in group]
    owner = [r for r, group in enumerate(groups) for _ in group]
    half, width = flat[0].shape
    for i, gradient in enumerate(flat):
        high, low = split(gradient)
        lanes = slice(i * width, (i + 1) * width)
        rhs_ref[0:half, lanes] = high
        rhs_ref[half : 2 * half, lanes] = high
        rhs_ref[2 * half :, lanes] = low
    rhs = rhs_ref[:, : len(flat) * width]
    results = []
    for c_ref in c_refs:
        fields = c_ref.shape[0] // half
        totals = [None] * len(flat)
        for k0 in range(0, fields, per_step):
            product = jnp.dot(c_ref[k0 * half : (k0 + per_step) * half, :], rhs, preferred_element_type=F32)
            for k in range(per_step):
                for i in range(len(flat)):
                    part = product[k * half : (k + 1) * half, i * width : (i + 1) * width]
                    part = part * weights[owner[i]][k0 + k : k0 + k + 1, :]
                    totals[i] = part if totals[i] is None else totals[i] + part
        results.append(totals)
    return results


def flux_kernel(count, plan, me_ref, w_ref, *refs):
    tasks, dense_keys, sources, behind, sums_in, final, carried, edges = plan
    me = me_ref[0]
    refs = list(refs)
    dense = {key: refs.pop(0) for key in dense_keys}
    w_behind = refs.pop(0) if behind else None
    ins = [[refs.pop(0) for _ in range(number)] for _, _, number, _ in sources]
    sums = {key: refs.pop(0) for key in sums_in}
    outs = [refs.pop(0) for _ in range(count // 2 if final else 0)]
    total = {key: refs.pop(0) for key in carried}
    edge_refs = [refs.pop(0) for _ in edges]
    planes_ref, rhs_ref = refs.pop(0), refs.pop(0)
    for key in final:
        total[key] = refs.pop(0)
    _, full_rows, half_modes, width = planes_ref.shape
    rows = full_rows - 1
    slot = {}
    for (plane, half, _, index), group in zip(sources, ins):
        here = slot[plane, half] = len(slot)
        if len(group) == 1:
            planes_ref[here, :rows] = group[0][:, half * half_modes : (half + 1) * half_modes, :]
        else:
            for i, ref in enumerate(group):
                planes_ref[here, :, half_row(me, i + half * count // 2, count, ref.shape[2]), :] = ref[index]
    for ref, key in zip(edge_refs, edges):
        ref[...] = planes_ref[slot[key], :rows]
    for key, ref in total.items():
        ref[...] = sums[key][...] if key in sums else jnp.zeros_like(ref)

    for plane, directions, half, sides in tasks:
        per_step = 2 if len(directions) > 1 else 4

        def step(i, carry, plane=plane, directions=directions, half=half, sides=sides, per_step=per_step):
            groups, weights = [], []
            for j in range(per_step):
                y = per_step * i + j
                here = planes_ref[slot[plane, half], y]
                group = []
                if "x" in directions:
                    group.append(ahead_x(here) - here)
                if "y" in directions:
                    group.append(planes_ref[slot[plane, half], y + 1] - here)
                if "z" in directions:
                    group.append(planes_ref[slot[plane + 1, half], y] - here)
                groups.append(group)
                weights.append(w_behind[0, y] if plane < 0 else w_ref[plane, y])
            results = couple([dense[half, side] for side in sides], rhs_ref, groups, weights, 4)
            for side, fluxes in zip(sides, results):
                here = total.get((plane, side))
                above = total.get((plane + 1, side))
                for j in range(per_step):
                    y = per_step * i + j
                    change = None
                    for direction in directions:
                        flux = fluxes.pop(0)
                        part = behind_x(flux) - flux if direction == "x" else -flux
                        change = part if change is None else change + part
                        if direction == "y":
                            here[y + 1] += flux
                        if direction == "z" and above is not None:
                            above[y] += flux
                    if here is not None:
                        here[y] += change
            return carry

        lax.fori_loop(0, rows // per_step, step, 0)
    side = final[0][1] if final else 0
    for i, out in enumerate(outs):
        for z, key in enumerate(final):
            out[z] = total[key][:, half_row(me, i + side * count // 2, count, out.shape[2]), :]


def fluxes(me, dense, weights, behind, tasks, sources, sums, final, carried, count, edges=(), busy=True):
    _, rows, fields, width = weights.shape
    half_modes = dense[0, 0].shape[0] // fields
    dense_keys = tuple(sorted({(half, side) for _, _, half, sides in tasks for side in sides}))
    needed = {(p, h) for p, _, h, _ in tasks} | {(p + 1, h) for p, directions, h, _ in tasks if "z" in directions}
    needed = sorted(needed | set(edges))
    listed = tuple((p, h, len(sources[p, h][0]), sources[p, h][1]) for p, h in needed)
    plan = (tasks, dense_keys, listed, behind is not None, tuple(sums), final, carried, edges)
    args = [weights] + [dense[key] for key in dense_keys] + ([] if behind is None else [behind])
    args += [array for key in needed for array in sources[key][0]] + list(sums.values())
    whole = (rows + 1, half_modes, width)
    piece = jax.ShapeDtypeStruct((len(final), rows + 1, 2 * half_modes // count, width), F32)
    out_shape = [piece] * (count // 2 if final else 0)
    number_out = len(out_shape)
    out_shape += [jax.ShapeDtypeStruct(whole, F32)] * len(carried)
    out_shape += [jax.ShapeDtypeStruct((rows, half_modes, width), F32)] * len(edges)
    scratch = [pltpu.VMEM((len(listed),) + whole, F32), pltpu.VMEM((3 * half_modes, 6 * width), BF16)]
    scratch += [pltpu.VMEM(whole, F32)] * len(final)
    units = rows * sum(len(directions) * len(sides) for _, directions, _, sides in tasks)
    results = pl.pallas_call(
        functools.partial(flux_kernel, count, plan),
        in_specs=[SMEM] + [VMEM] * len(args),
        out_specs=[VMEM] * len(out_shape),
        out_shape=out_shape,
        scratch_shapes=scratch,
        compiler_params=params(32),
        cost_estimate=cost(busy * units * 4 * dense[0, 0].shape[0] * 2 * half_modes * width, 1),
        name="fluxes_" + "_".join(f"{p}{directions}{half}" for p, directions, half, _ in tasks),
    )(me, *args)
    sums_out = dict(zip(carried, results[number_out:]))
    return results[:number_out], sums_out, results[number_out + len(carried) :]


def unpack_kernel(count, chunks, me_ref, *refs):
    me = me_ref[0]
    step = pl.program_id(0)
    out = refs[-1]
    for c, planes in enumerate(chunks):
        chosen = functools.reduce(lambda left, right: left | right, [step == plane for plane in planes])

        @pl.when(chosen)
        def _(ins=refs[c * count : (c + 1) * count]):
            rows = ins[0].shape[1] - 1
            for s, ref in enumerate(ins):
                out[:, 0, part_of(me ^ s, rows), :] = jnp.swapaxes(ref[0, :rows], 0, 1)
            for s, ref in enumerate(ins):
                owner = me ^ s
                there = part_of(after(owner, count), rows)
                added = jnp.where(owner < count - 1, ref[0, rows], 0.0)[:, None, :]
                value = out[:, 0, there, :]
                row = lax.broadcasted_iota(jnp.int32, value.shape, 1)
                out[:, 0, there, :] = value + jnp.where(row == 0, added, 0.0)


def unpack(me, received, chunks, shape):
    modes, depth, height, width = shape
    count = len(received[0])
    in_specs, args = [SMEM], [me]
    for planes, pieces in zip(chunks, received):

        def place(i, planes=planes):
            return (functools.reduce(jnp.add, [(i >= plane).astype(jnp.int32) for plane in planes[1:]], 0), 0, 0, 0)

        in_specs += [pl.BlockSpec((1,) + pieces[0].shape[1:], place)] * count
        args += list(pieces)
    return pl.pallas_call(
        functools.partial(unpack_kernel, count, chunks),
        grid=(depth,),
        in_specs=in_specs,
        out_specs=pl.BlockSpec((modes, 1, height, width), lambda i: (0, i, 0, 0)),
        out_shape=jax.ShapeDtypeStruct(shape, F32),
        compiler_params=params(16),
        cost_estimate=cost(1, 1),
        name="unpack",
    )(*args)


def body(field, coefficient_fields, triple_blocks, block_pattern):
    count = lax.axis_size("mode")
    depth = field.shape[1]
    top = depth - 1
    me = lax.axis_index("mode").astype(jnp.int32).reshape(1)
    near, far = tuple(range(1, count // 2)), tuple(range(count // 2, count))
    forth = far[:1] + near + far[1:]

    sent = exchange(pack(me, field, count), forth)
    dense, weights = prepare(me, triple_blocks, block_pattern, coefficient_fields, count)
    weights_behind = from_behind(weights[top:], "slab", 1)
    sides = (sent[: count // 2], sent[count // 2 :])
    sources = {(p, h): (sides[h], p) for p in range(depth) for h in (0, 1)}

    def add(*args, **options):
        return fluxes(me, dense, weights, *args, count, **options)

    def keys(side):
        return tuple((p, side) for p in range(depth))

    def inside(half, to):
        return tuple((p, "xyz", half, to) for p in range(top)) + ((top, "xy", half, to),)

    def outside(to):
        return tuple((p, "z", half, to) for half in (0, 1) for p in (top, -1))

    _, sums, near_ends = add(None, inside(0, (0, 1)), sources, {}, (), keys(0) + keys(1), edges=((0, 0), (top, 0)), busy=False)
    lowest, highest = edges(me, near_ends, sides[1], (0, top), count)
    above = from_behind(lowest, "slab", -1)
    below = from_behind(highest, "slab", 1)
    for half in (0, 1):
        sources[depth, half] = ([above], 0)
        sources[-1, half] = ([below], 0)
    _, far_sums, _ = add(None, inside(1, (1,)), sources, {key: sums[key] for key in keys(1)}, (), keys(1))
    far_pieces, _, _ = add(weights_behind, outside((1,)), sources, far_sums, keys(1), ())
    near_sums = {key: sums[key] for key in keys(0)}
    near_pieces, _, _ = add(weights_behind, inside(1, (0,)) + outside((0,)), sources, near_sums, keys(0), ())
    back = exchange(list(near_pieces) + list(far_pieces), far + near)
    return unpack(me, (back,), (tuple(range(depth)),), field.shape)


def solution(mesh):
    in_specs = (P("mode", "slab", None, None), P(None, "slab", "mode", None), P(), P())
    out_specs = P("mode", "slab", None, None)
    return jax.shard_map(body, mesh=mesh, in_specs=in_specs, out_specs=out_specs, check_vma=False)
```

```python
import functools

import jax
import jax.numpy as jnp
from jax import lax
from jax.experimental import pallas as pl
from jax.experimental.pallas import tpu as pltpu
from jax.sharding import PartitionSpec as P

F32 = jnp.float32
BF16 = jnp.bfloat16
VMEM = pl.BlockSpec(memory_space=pltpu.VMEM)
SMEM = pl.BlockSpec(memory_space=pltpu.SMEM)
MIB = 2**20


def params(mib):
    return pltpu.CompilerParams(vmem_limit_bytes=mib * MIB)


def cost(flops, size):
    return pl.CostEstimate(flops=int(flops), bytes_accessed=int(size), transcendentals=0)


def from_behind(value, axis, steps):
    count = lax.axis_size(axis)
    first, last = (max(0, -steps), min(count, count - steps))
    return lax.ppermute(value, axis, [(source, source + steps) for source in range(first, last)])


def exchange(pieces, order):
    count = len(pieces)
    received = list(pieces)
    for s in order:
        received[s] = lax.ppermute(pieces[s], "mode", [(i, i ^ s) for i in range(count)])
    return received


def part_of(owner, size):
    return pl.ds(pl.multiple_of(owner * size, size), size)


def after(owner, count):
    return jnp.minimum(owner + 1, count - 1)


def split(value):
    high = value.astype(BF16)
    return high, (value - high.astype(F32)).astype(BF16)


def prepare_kernel(count, me_ref, pattern_ref, blocks_ref, field_ref, *outs):
    dense_refs, weights_ref = outs[:4], outs[4]
    fields, row_blocks, block, stored = blocks_ref.shape
    modes = row_blocks * block
    half = modes // 2
    lane = lax.broadcasted_iota(jnp.int32, (block, modes), 1)
    side = me_ref[0] // (count // 2)

    def one_field(k, carry):
        for j in range(row_blocks):
            rows_side, local = divmod(j, row_blocks // 2)
            r = (side ^ rows_side) * (row_blocks // 2) + local
            value = blocks_ref[k, r]
            value = jnp.concatenate([value, jnp.zeros((block, modes - stored), F32)], axis=1)
            total = None
            for c in range(stored // block):
                part = jnp.where((lane >= c * block) & (lane < (c + 1) * block), value, 0.0)
                shift = lax.rem(pattern_ref[k, r, c] - c + row_blocks, row_blocks) * block
                part = pltpu.roll(part, shift, 1)
                total = part if total is None else total + part
            total = pltpu.roll(total, side * half, 1)
            high, low = (part.astype(F32) for part in split(total))
            other_high, other_low = pltpu.roll(high, half, 1), pltpu.roll(low, half, 1)
            rows = pl.ds(pl.multiple_of(k * half + local * block, block), block)
            near = jnp.where(lane < half, high, other_low).astype(BF16), high[:, :half].astype(BF16)
            far = jnp.where(lane < half, other_high, low).astype(BF16), other_high[:, :half].astype(BF16)
            for columns_side, parts in enumerate((near, far)):
                dense_refs[2 * columns_side + rows_side][rows, 0:modes] = parts[0]
                dense_refs[2 * columns_side + rows_side][rows, modes:] = parts[1]
        return carry

    lax.fori_loop(0, fields, one_field, 0)
    for z in range(weights_ref.shape[0]):
        weights_ref[z] = jnp.swapaxes(field_ref[:, z], 0, 1)


def prepare(me, triple_blocks, block_pattern, coefficient_fields, count):
    fields, row_blocks, block, _ = triple_blocks.shape
    modes = row_blocks * block
    _, depth, rows, width = coefficient_fields.shape
    part = jax.ShapeDtypeStruct((fields * modes // 2, 3 * modes // 2), BF16)
    *parts, weights = pl.pallas_call(
        functools.partial(prepare_kernel, count),
        in_specs=[SMEM, SMEM, VMEM, VMEM],
        out_specs=[VMEM] * 5,
        out_shape=[part] * 4 + [jax.ShapeDtypeStruct((depth, rows, fields, width), F32)],
        compiler_params=params(16),
        cost_estimate=cost(1, 1),
        name="prepare",
    )(me, block_pattern, triple_blocks, coefficient_fields)
    return {(i // 2, i % 2): part for i, part in enumerate(parts)}, weights


def pack_kernel(count, me_ref, field_ref, *outs):
    me = me_ref[0]
    rows = field_ref.shape[2] // count
    for s, out in enumerate(outs):
        owner = me ^ s
        own = field_ref[:, 0, part_of(owner, rows), :]
        out[0, :rows] = jnp.swapaxes(own, 0, 1)
        ahead = field_ref[:, 0, part_of(after(owner, count), rows), :][:, 0]
        out[0, rows] = jnp.where(owner < count - 1, ahead, 0.0)


def pack(me, field, count):
    modes, depth, height, width = field.shape
    rows = height // count
    block = (1, rows + 1, modes, width)
    return pl.pallas_call(
        functools.partial(pack_kernel, count),
        grid=(depth,),
        in_specs=[SMEM, pl.BlockSpec((modes, 1, height, width), lambda i: (0, i, 0, 0))],
        out_specs=[pl.BlockSpec(block, lambda i: (i, 0, 0, 0))] * count,
        out_shape=[jax.ShapeDtypeStruct((depth,) + block[1:], F32)] * count,
        compiler_params=params(16),
        cost_estimate=cost(1, 1),
        name="pack",
    )(me, field)


def half_row(me, s, count, size):
    return part_of((me ^ s) & (count // 2 - 1), size)


def ahead_x(value):
    width = value.shape[-1]
    lane = lax.broadcasted_iota(jnp.int32, value.shape, 1)
    return jnp.where(lane == width - 1, 0.0, pltpu.roll(value, width - 1, 1))


def behind_x(value):
    lane = lax.broadcasted_iota(jnp.int32, value.shape, 1)
    return jnp.where(lane == 0, 0.0, pltpu.roll(value, 1, 1))


def edges_kernel(count, picks, me_ref, *refs):
    me = me_ref[0]
    near, far, outs = refs[: len(picks)], refs[len(picks) : len(picks) + count // 2], refs[len(picks) + count // 2 :]
    for out, own, index in zip(outs, near, picks):
        rows, modes, _ = out.shape
        out[:, : modes // 2, :] = own[...]
        for i, ref in enumerate(far):
            size = ref.shape[2]
            start = modes // 2 + ((me ^ (i + count // 2)) & (count // 2 - 1)) * size
            out[:, pl.ds(pl.multiple_of(start, size), size), :] = ref[index, :rows]


def edges(me, near, far, picks, count):
    rows, half, width = near[0].shape
    return pl.pallas_call(
        functools.partial(edges_kernel, count, picks),
        in_specs=[SMEM] + [VMEM] * (len(near) + len(far)),
        out_specs=[VMEM] * len(picks),
        out_shape=[jax.ShapeDtypeStruct((rows, 2 * half, width), F32)] * len(picks),
        compiler_params=params(16),
        cost_estimate=cost(1, 1),
        name="edges",
    )(me, *near, *far)


def couple(c_refs, rhs_ref, groups, weights, per_step):
    flat = [gradient for group in groups for gradient in group]
    owner = [r for r, group in enumerate(groups) for _ in group]
    half, width = flat[0].shape
    for i, gradient in enumerate(flat):
        high, low = split(gradient)
        lanes = slice(i * width, (i + 1) * width)
        rhs_ref[0:half, lanes] = high
        rhs_ref[half : 2 * half, lanes] = high
        rhs_ref[2 * half :, lanes] = low
    rhs = rhs_ref[:, : len(flat) * width]
    results = []
    for c_ref in c_refs:
        fields = c_ref.shape[0] // half
        totals = [None] * len(flat)
        for k0 in range(0, fields, per_step):
            product = jnp.dot(c_ref[k0 * half : (k0 + per_step) * half, :], rhs, preferred_element_type=F32)
            for k in range(per_step):
                for i in range(len(flat)):
                    part = product[k * half : (k + 1) * half, i * width : (i + 1) * width]
                    part = part * weights[owner[i]][k0 + k : k0 + k + 1, :]
                    totals[i] = part if totals[i] is None else totals[i] + part
        results.append(totals)
    return results


def flux_kernel(count, plan, me_ref, w_ref, *refs):
    tasks, dense_keys, sources, behind, sums_in, final, carried, edges = plan
    me = me_ref[0]
    refs = list(refs)
    dense = {key: refs.pop(0) for key in dense_keys}
    w_behind = refs.pop(0) if behind else None
    ins = [[refs.pop(0) for _ in range(number)] for _, _, number, _ in sources]
    sums = {key: refs.pop(0) for key in sums_in}
    outs = [refs.pop(0) for _ in range(count // 2 if final else 0)]
    total = {key: refs.pop(0) for key in carried}
    edge_refs = [refs.pop(0) for _ in edges]
    planes_ref, rhs_ref = refs.pop(0), refs.pop(0)
    for key in final:
        total[key] = refs.pop(0)
    _, full_rows, half_modes, width = planes_ref.shape
    rows = full_rows - 1
    slot = {}
    for (plane, half, _, index), group in zip(sources, ins):
        here = slot[plane, half] = len(slot)
        if len(group) == 1:
            planes_ref[here, :rows] = group[0][:, half * half_modes : (half + 1) * half_modes, :]
        else:
            for i, ref in enumerate(group):
                planes_ref[here, :, half_row(me, i + half * count // 2, count, ref.shape[2]), :] = ref[index]
    for ref, key in zip(edge_refs, edges):
        ref[...] = planes_ref[slot[key], :rows]
    for key, ref in total.items():
        ref[...] = sums[key][...] if key in sums else jnp.zeros_like(ref)

    for plane, directions, half, sides in tasks:
        per_step = rows

        def step(i, carry, plane=plane, directions=directions, half=half, sides=sides, per_step=per_step):
            groups, weights = [], []
            for j in range(per_step):
                y = per_step * i + j
                here = planes_ref[slot[plane, half], y]
                group = []
                if "x" in directions:
                    group.append(ahead_x(here) - here)
                if "y" in directions:
                    group.append(planes_ref[slot[plane, half], y + 1] - here)
                if "z" in directions:
                    group.append(planes_ref[slot[plane + 1, half], y] - here)
                groups.append(group)
                weights.append(w_behind[0, y] if plane < 0 else w_ref[plane, y])
            results = couple([dense[half, side] for side in sides], rhs_ref, groups, weights, 4)
            for side, fluxes in zip(sides, results):
                here = total.get((plane, side))
                above = total.get((plane + 1, side))
                for j in range(per_step):
                    y = per_step * i + j
                    change = None
                    for direction in directions:
                        flux = fluxes.pop(0)
                        part = behind_x(flux) - flux if direction == "x" else -flux
                        change = part if change is None else change + part
                        if direction == "y":
                            here[y + 1] += flux
                        if direction == "z" and above is not None:
                            above[y] += flux
                    if here is not None:
                        here[y] += change
            return carry

        lax.fori_loop(0, rows // per_step, step, 0)
    side = final[0][1] if final else 0
    for i, out in enumerate(outs):
        for z, key in enumerate(final):
            out[z] = total[key][:, half_row(me, i + side * count // 2, count, out.shape[2]), :]


def fluxes(me, dense, weights, behind, tasks, sources, sums, final, carried, count, edges=(), busy=True):
    _, rows, fields, width = weights.shape
    half_modes = dense[0, 0].shape[0] // fields
    dense_keys = tuple(sorted({(half, side) for _, _, half, sides in tasks for side in sides}))
    needed = {(p, h) for p, _, h, _ in tasks} | {(p + 1, h) for p, directions, h, _ in tasks if "z" in directions}
    needed = sorted(needed | set(edges))
    listed = tuple((p, h, len(sources[p, h][0]), sources[p, h][1]) for p, h in needed)
    plan = (tasks, dense_keys, listed, behind is not None, tuple(sums), final, carried, edges)
    args = [weights] + [dense[key] for key in dense_keys] + ([] if behind is None else [behind])
    args += [array for key in needed for array in sources[key][0]] + list(sums.values())
    whole = (rows + 1, half_modes, width)
    piece = jax.ShapeDtypeStruct((len(final), rows + 1, 2 * half_modes // count, width), F32)
    out_shape = [piece] * (count // 2 if final else 0)
    number_out = len(out_shape)
    out_shape += [jax.ShapeDtypeStruct(whole, F32)] * len(carried)
    out_shape += [jax.ShapeDtypeStruct((rows, half_modes, width), F32)] * len(edges)
    scratch = [pltpu.VMEM((len(listed),) + whole, F32), pltpu.VMEM((3 * half_modes, 3 * rows * width), BF16)]
    scratch += [pltpu.VMEM(whole, F32)] * len(final)
    units = rows * sum(len(directions) * len(sides) for _, directions, _, sides in tasks)
    results = pl.pallas_call(
        functools.partial(flux_kernel, count, plan),
        in_specs=[SMEM] + [VMEM] * len(args),
        out_specs=[VMEM] * len(out_shape),
        out_shape=out_shape,
        scratch_shapes=scratch,
        compiler_params=params(32),
        cost_estimate=cost(busy * units * 4 * dense[0, 0].shape[0] * 2 * half_modes * width, 1),
        name="fluxes_" + "_".join(f"{p}{directions}{half}" for p, directions, half, _ in tasks),
    )(me, *args)
    sums_out = dict(zip(carried, results[number_out:]))
    return results[:number_out], sums_out, results[number_out + len(carried) :]


def unpack_kernel(count, chunks, me_ref, *refs):
    me = me_ref[0]
    step = pl.program_id(0)
    out = refs[-1]
    for c, planes in enumerate(chunks):
        chosen = functools.reduce(lambda left, right: left | right, [step == plane for plane in planes])

        @pl.when(chosen)
        def _(ins=refs[c * count : (c + 1) * count][::-1]):
            rows = ins[0].shape[1] - 1
            for s, ref in enumerate(ins):
                out[:, 0, part_of(me ^ s, rows), :] = jnp.swapaxes(ref[0, :rows], 0, 1)
            for s, ref in enumerate(ins):
                owner = me ^ s
                there = part_of(after(owner, count), rows)
                added = jnp.where(owner < count - 1, ref[0, rows], 0.0)[:, None, :]
                value = out[:, 0, there, :]
                row = lax.broadcasted_iota(jnp.int32, value.shape, 1)
                out[:, 0, there, :] = value + jnp.where(row == 0, added, 0.0)


def unpack(me, received, chunks, shape):
    modes, depth, height, width = shape
    count = len(received[0])
    in_specs, args = [SMEM], [me]
    for planes, pieces in zip(chunks, received):

        def place(i, planes=planes):
            return (functools.reduce(jnp.add, [(i >= plane).astype(jnp.int32) for plane in planes[1:]], 0), 0, 0, 0)

        in_specs += [pl.BlockSpec((1,) + pieces[0].shape[1:], place)] * count
        args += list(pieces)[::-1]
    return pl.pallas_call(
        functools.partial(unpack_kernel, count, chunks),
        grid=(depth,),
        in_specs=in_specs,
        out_specs=pl.BlockSpec((modes, 1, height, width), lambda i: (0, i, 0, 0)),
        out_shape=jax.ShapeDtypeStruct(shape, F32),
        compiler_params=params(16),
        cost_estimate=cost(1, 1),
        name="unpack",
    )(*args)


def body(field, coefficient_fields, triple_blocks, block_pattern):
    count = lax.axis_size("mode")
    depth = field.shape[1]
    top = depth - 1
    me = lax.axis_index("mode").astype(jnp.int32).reshape(1)
    near, far = tuple(range(1, count // 2)), tuple(range(count // 2, count))
    forth = far[:1] + near + far[1:]

    sent = exchange(pack(me, field, count), forth)
    dense, weights = prepare(me, triple_blocks, block_pattern, coefficient_fields, count)
    weights_behind = from_behind(weights[top:], "slab", 1)
    sides = (sent[: count // 2], sent[count // 2 :])
    sources = {(p, h): (sides[h], p) for p in range(depth) for h in (0, 1)}

    def add(*args, **options):
        return fluxes(me, dense, weights, *args, count, **options)

    def keys(side):
        return tuple((p, side) for p in range(depth))

    def inside(half, to):
        return tuple((p, "xyz", half, to) for p in range(top)) + ((top, "xy", half, to),)

    def outside(to):
        return tuple((p, "z", half, to) for half in (0, 1) for p in (top, -1))

    _, sums, near_ends = add(None, inside(0, (0, 1)), sources, {}, (), keys(0) + keys(1), edges=((0, 0), (top, 0)), busy=False)
    lowest, highest = edges(me, near_ends, sides[1], (0, top), count)
    above = from_behind(lowest, "slab", -1)
    below = from_behind(highest, "slab", 1)
    for half in (0, 1):
        sources[depth, half] = ([above], 0)
        sources[-1, half] = ([below], 0)
    _, far_sums, _ = add(None, inside(1, (1,)), sources, {key: sums[key] for key in keys(1)}, (), keys(1))
    far_pieces, _, _ = add(weights_behind, outside((1,)), sources, far_sums, keys(1), ())
    near_sums = {key: sums[key] for key in keys(0)}
    near_pieces, _, _ = add(weights_behind, inside(1, (0,)) + outside((0,)), sources, near_sums, keys(0), ())
    back = exchange(list(near_pieces) + list(far_pieces), far + near)
    return unpack(me, (back,), (tuple(range(depth)),), field.shape)


def solution(mesh):
    in_specs = (P("mode", "slab", None, None), P(None, "slab", "mode", None), P(), P())
    out_specs = P("mode", "slab", None, None)
    return jax.shard_map(body, mesh=mesh, in_specs=in_specs, out_specs=out_specs, check_vma=False)
```

```python
import functools

import jax
import jax.numpy as jnp
from jax import lax
from jax.experimental import pallas as pl
from jax.experimental.pallas import tpu as pltpu
from jax.sharding import PartitionSpec as P

F32 = jnp.float32
BF16 = jnp.bfloat16
VMEM = pl.BlockSpec(memory_space=pltpu.VMEM)
SMEM = pl.BlockSpec(memory_space=pltpu.SMEM)
MIB = 2**20


def params(mib):
    return pltpu.CompilerParams(vmem_limit_bytes=mib * MIB)


def cost(flops, size):
    return pl.CostEstimate(flops=int(flops), bytes_accessed=int(size), transcendentals=0)


def from_behind(value, axis, steps):
    count = lax.axis_size(axis)
    first, last = (max(0, -steps), min(count, count - steps))
    return lax.ppermute(value, axis, [(source, source + steps) for source in range(first, last)])


def exchange(pieces, order):
    count = len(pieces)
    received = list(pieces)
    for s in order:
        received[s] = lax.ppermute(pieces[s], "mode", [(i, i ^ s) for i in range(count)])
    return received


def part_of(owner, size):
    return pl.ds(pl.multiple_of(owner * size, size), size)


def after(owner, count):
    return jnp.minimum(owner + 1, count - 1)


def split(value):
    high = value.astype(BF16)
    return high, (value - high.astype(F32)).astype(BF16)


def prepare_kernel(count, me_ref, pattern_ref, blocks_ref, field_ref, *outs):
    dense_refs, weights_ref = outs[:4], outs[4]
    fields, row_blocks, block, stored = blocks_ref.shape
    modes = row_blocks * block
    half = modes // 2
    lane = lax.broadcasted_iota(jnp.int32, (block, modes), 1)
    side = me_ref[0] // (count // 2)

    def one_field(k, carry):
        for j in range(row_blocks):
            rows_side, local = divmod(j, row_blocks // 2)
            r = (side ^ rows_side) * (row_blocks // 2) + local
            value = blocks_ref[k, r]
            value = jnp.concatenate([value, jnp.zeros((block, modes - stored), F32)], axis=1)
            total = None
            for c in range(stored // block):
                part = jnp.where((lane >= c * block) & (lane < (c + 1) * block), value, 0.0)
                shift = lax.rem(pattern_ref[k, r, c] - c + row_blocks, row_blocks) * block
                part = pltpu.roll(part, shift, 1)
                total = part if total is None else total + part
            total = pltpu.roll(total, side * half, 1)
            high, low = (part.astype(F32) for part in split(total))
            other_high, other_low = pltpu.roll(high, half, 1), pltpu.roll(low, half, 1)
            rows = pl.ds(pl.multiple_of(k * half + local * block, block), block)
            near = jnp.where(lane < half, high, other_low).astype(BF16), high[:, :half].astype(BF16)
            far = jnp.where(lane < half, other_high, low).astype(BF16), other_high[:, :half].astype(BF16)
            for columns_side, parts in enumerate((near, far)):
                dense_refs[2 * columns_side + rows_side][rows, 0:modes] = parts[0]
                dense_refs[2 * columns_side + rows_side][rows, modes:] = parts[1]
        return carry

    lax.fori_loop(0, fields, one_field, 0)
    for z in range(weights_ref.shape[0]):
        weights_ref[z] = jnp.swapaxes(field_ref[:, z], 0, 1)


def prepare(me, triple_blocks, block_pattern, coefficient_fields, count):
    fields, row_blocks, block, _ = triple_blocks.shape
    modes = row_blocks * block
    _, depth, rows, width = coefficient_fields.shape
    part = jax.ShapeDtypeStruct((fields * modes // 2, 3 * modes // 2), BF16)
    *parts, weights = pl.pallas_call(
        functools.partial(prepare_kernel, count),
        in_specs=[SMEM, SMEM, VMEM, VMEM],
        out_specs=[VMEM] * 5,
        out_shape=[part] * 4 + [jax.ShapeDtypeStruct((depth, rows, fields, width), F32)],
        compiler_params=params(16),
        cost_estimate=cost(1, 1),
        name="prepare",
    )(me, block_pattern, triple_blocks, coefficient_fields)
    return {(i // 2, i % 2): part for i, part in enumerate(parts)}, weights


def pack_kernel(count, me_ref, field_ref, *outs):
    me = me_ref[0]
    rows = field_ref.shape[2] // count
    for s, out in enumerate(outs):
        owner = me ^ s
        own = field_ref[:, 0, part_of(owner, rows), :]
        out[0, :rows] = jnp.swapaxes(own, 0, 1)
        ahead = field_ref[:, 0, part_of(after(owner, count), rows), :][:, 0]
        out[0, rows] = jnp.where(owner < count - 1, ahead, 0.0)


def pack(me, field, count):
    modes, depth, height, width = field.shape
    rows = height // count
    block = (1, rows + 1, modes, width)
    return pl.pallas_call(
        functools.partial(pack_kernel, count),
        grid=(depth,),
        in_specs=[SMEM, pl.BlockSpec((modes, 1, height, width), lambda i: (0, i, 0, 0))],
        out_specs=[pl.BlockSpec(block, lambda i: (i, 0, 0, 0))] * count,
        out_shape=[jax.ShapeDtypeStruct((depth,) + block[1:], F32)] * count,
        compiler_params=params(16),
        cost_estimate=cost(1, 1),
        name="pack",
    )(me, field)


def half_row(me, s, count, size):
    return part_of((me ^ s) & (count // 2 - 1), size)


def ahead_x(value):
    width = value.shape[-1]
    lane = lax.broadcasted_iota(jnp.int32, value.shape, 1)
    return jnp.where(lane == width - 1, 0.0, pltpu.roll(value, width - 1, 1))


def behind_x(value):
    lane = lax.broadcasted_iota(jnp.int32, value.shape, 1)
    return jnp.where(lane == 0, 0.0, pltpu.roll(value, 1, 1))


def edges_kernel(count, picks, me_ref, *refs):
    me = me_ref[0]
    near, far, outs = refs[: len(picks)], refs[len(picks) : len(picks) + count // 2], refs[len(picks) + count // 2 :]
    for out, own, index in zip(outs, near, picks):
        rows, modes, _ = out.shape
        out[:, : modes // 2, :] = own[...]
        for i, ref in enumerate(far):
            size = ref.shape[2]
            start = modes // 2 + ((me ^ (i + count // 2)) & (count // 2 - 1)) * size
            out[:, pl.ds(pl.multiple_of(start, size), size), :] = ref[index, :rows]


def edges(me, near, far, picks, count):
    rows, half, width = near[0].shape
    return pl.pallas_call(
        functools.partial(edges_kernel, count, picks),
        in_specs=[SMEM] + [VMEM] * (len(near) + len(far)),
        out_specs=[VMEM] * len(picks),
        out_shape=[jax.ShapeDtypeStruct((rows, 2 * half, width), F32)] * len(picks),
        compiler_params=params(16),
        cost_estimate=cost(1, 1),
        name="edges",
    )(me, *near, *far)


def couple(c_refs, rhs_ref, groups, weights, per_step):
    flat = [gradient for group in groups for gradient in group]
    owner = [r for r, group in enumerate(groups) for _ in group]
    half, width = flat[0].shape
    for i, gradient in enumerate(flat):
        high, low = split(gradient)
        lanes = slice(i * width, (i + 1) * width)
        rhs_ref[0:half, lanes] = high
        rhs_ref[half : 2 * half, lanes] = high
        rhs_ref[2 * half :, lanes] = low
    rhs = rhs_ref[:, : len(flat) * width]
    results = []
    for c_ref in c_refs:
        fields = c_ref.shape[0] // half
        totals = [None] * len(flat)
        for k0 in range(0, fields, per_step):
            product = jnp.dot(c_ref[k0 * half : (k0 + per_step) * half, :], rhs, preferred_element_type=F32)
            for k in range(per_step):
                for i in range(len(flat)):
                    part = product[k * half : (k + 1) * half, i * width : (i + 1) * width]
                    part = part * weights[owner[i]][k0 + k : k0 + k + 1, :]
                    totals[i] = part if totals[i] is None else totals[i] + part
        results.append(totals)
    return results


def flux_kernel(count, plan, me_ref, w_ref, *refs):
    tasks, dense_keys, sources, behind, sums_in, final, carried, edges = plan
    me = me_ref[0]
    refs = list(refs)
    dense = {key: refs.pop(0) for key in dense_keys}
    w_behind = refs.pop(0) if behind else None
    ins = [[refs.pop(0) for _ in range(number)] for _, _, number, _ in sources]
    sums = {key: refs.pop(0) for key in sums_in}
    outs = [refs.pop(0) for _ in range(count // 2 if final else 0)]
    total = {key: refs.pop(0) for key in carried}
    edge_refs = [refs.pop(0) for _ in edges]
    planes_ref, rhs_ref = refs.pop(0), refs.pop(0)
    for key in final:
        total[key] = refs.pop(0)
    _, full_rows, half_modes, width = planes_ref.shape
    rows = full_rows - 1
    slot = {}
    for (plane, half, _, index), group in zip(sources, ins):
        here = slot[plane, half] = len(slot)
        if len(group) == 1:
            planes_ref[here, :rows] = group[0][:, half * half_modes : (half + 1) * half_modes, :]
        else:
            for i, ref in enumerate(group):
                planes_ref[here, :, half_row(me, i + half * count // 2, count, ref.shape[2]), :] = ref[index]
    for ref, key in zip(edge_refs, edges):
        ref[...] = planes_ref[slot[key], :rows]
    for key, ref in total.items():
        ref[...] = sums[key][...] if key in sums else jnp.zeros_like(ref)

    for plane, directions, half, sides in tasks:
        per_step = 4 if len(directions) > 1 else 8

        def step(i, carry, plane=plane, directions=directions, half=half, sides=sides, per_step=per_step):
            groups, weights = [], []
            for j in range(per_step):
                y = per_step * i + j
                here = planes_ref[slot[plane, half], y]
                group = []
                if "x" in directions:
                    group.append(ahead_x(here) - here)
                if "y" in directions:
                    group.append(planes_ref[slot[plane, half], y + 1] - here)
                if "z" in directions:
                    group.append(planes_ref[slot[plane + 1, half], y] - here)
                groups.append(group)
                weights.append(w_behind[0, y] if plane < 0 else w_ref[plane, y])
            results = couple([dense[half, side] for side in sides], rhs_ref, groups, weights, 4)
            for side, fluxes in zip(sides, results):
                here = total.get((plane, side))
                above = total.get((plane + 1, side))
                for j in range(per_step):
                    y = per_step * i + j
                    change = None
                    for direction in directions:
                        flux = fluxes.pop(0)
                        part = behind_x(flux) - flux if direction == "x" else -flux
                        change = part if change is None else change + part
                        if direction == "y":
                            here[y + 1] += flux
                        if direction == "z" and above is not None:
                            above[y] += flux
                    if here is not None:
                        here[y] += change
            return carry

        lax.fori_loop(0, rows // per_step, step, 0)
    side = final[0][1] if final else 0
    for i, out in enumerate(outs):
        for z, key in enumerate(final):
            out[z] = total[key][:, half_row(me, i + side * count // 2, count, out.shape[2]), :]


def fluxes(me, dense, weights, behind, tasks, sources, sums, final, carried, count, edges=(), busy=True):
    _, rows, fields, width = weights.shape
    half_modes = dense[0, 0].shape[0] // fields
    dense_keys = tuple(sorted({(half, side) for _, _, half, sides in tasks for side in sides}))
    needed = {(p, h) for p, _, h, _ in tasks} | {(p + 1, h) for p, directions, h, _ in tasks if "z" in directions}
    needed = sorted(needed | set(edges))
    listed = tuple((p, h, len(sources[p, h][0]), sources[p, h][1]) for p, h in needed)
    plan = (tasks, dense_keys, listed, behind is not None, tuple(sums), final, carried, edges)
    args = [weights] + [dense[key] for key in dense_keys] + ([] if behind is None else [behind])
    args += [array for key in needed for array in sources[key][0]] + list(sums.values())
    whole = (rows + 1, half_modes, width)
    piece = jax.ShapeDtypeStruct((len(final), rows + 1, 2 * half_modes // count, width), F32)
    out_shape = [piece] * (count // 2 if final else 0)
    number_out = len(out_shape)
    out_shape += [jax.ShapeDtypeStruct(whole, F32)] * len(carried)
    out_shape += [jax.ShapeDtypeStruct((rows, half_modes, width), F32)] * len(edges)
    scratch = [pltpu.VMEM((len(listed),) + whole, F32), pltpu.VMEM((3 * half_modes, 12 * width), BF16)]
    scratch += [pltpu.VMEM(whole, F32)] * len(final)
    units = rows * sum(len(directions) * len(sides) for _, directions, _, sides in tasks)
    results = pl.pallas_call(
        functools.partial(flux_kernel, count, plan),
        in_specs=[SMEM] + [VMEM] * len(args),
        out_specs=[VMEM] * len(out_shape),
        out_shape=out_shape,
        scratch_shapes=scratch,
        compiler_params=params(32),
        cost_estimate=cost(busy * units * 4 * dense[0, 0].shape[0] * 2 * half_modes * width, 1),
        name="fluxes_" + "_".join(f"{p}{directions}{half}" for p, directions, half, _ in tasks),
    )(me, *args)
    sums_out = dict(zip(carried, results[number_out:]))
    return results[:number_out], sums_out, results[number_out + len(carried) :]


def unpack_kernel(count, chunks, me_ref, *refs):
    me = me_ref[0]
    step = pl.program_id(0)
    out = refs[-1]
    for c, planes in enumerate(chunks):
        chosen = functools.reduce(lambda left, right: left | right, [step == plane for plane in planes])

        @pl.when(chosen)
        def _(ins=refs[c * count : (c + 1) * count][::-1]):
            rows = ins[0].shape[1] - 1
            for s, ref in enumerate(ins):
                out[:, 0, part_of(me ^ s, rows), :] = jnp.swapaxes(ref[0, :rows], 0, 1)
            for s, ref in enumerate(ins):
                owner = me ^ s
                there = part_of(after(owner, count), rows)
                added = jnp.where(owner < count - 1, ref[0, rows], 0.0)[:, None, :]
                value = out[:, 0, there, :]
                row = lax.broadcasted_iota(jnp.int32, value.shape, 1)
                out[:, 0, there, :] = value + jnp.where(row == 0, added, 0.0)


def unpack(me, received, chunks, shape):
    modes, depth, height, width = shape
    count = len(received[0])
    in_specs, args = [SMEM], [me]
    for planes, pieces in zip(chunks, received):

        def place(i, planes=planes):
            return (functools.reduce(jnp.add, [(i >= plane).astype(jnp.int32) for plane in planes[1:]], 0), 0, 0, 0)

        in_specs += [pl.BlockSpec((1,) + pieces[0].shape[1:], place)] * count
        args += list(pieces)[::-1]
    return pl.pallas_call(
        functools.partial(unpack_kernel, count, chunks),
        grid=(depth,),
        in_specs=in_specs,
        out_specs=pl.BlockSpec((modes, 1, height, width), lambda i: (0, i, 0, 0)),
        out_shape=jax.ShapeDtypeStruct(shape, F32),
        compiler_params=params(16),
        cost_estimate=cost(1, 1),
        name="unpack",
    )(*args)


def body(field, coefficient_fields, triple_blocks, block_pattern):
    count = lax.axis_size("mode")
    depth = field.shape[1]
    top = depth - 1
    me = lax.axis_index("mode").astype(jnp.int32).reshape(1)
    near, far = tuple(range(1, count // 2)), tuple(range(count // 2, count))
    forth = far[:1] + near + far[1:]

    sent = exchange(pack(me, field, count), forth)
    dense, weights = prepare(me, triple_blocks, block_pattern, coefficient_fields, count)
    weights_behind = from_behind(weights[top:], "slab", 1)
    sides = (sent[: count // 2], sent[count // 2 :])
    sources = {(p, h): (sides[h], p) for p in range(depth) for h in (0, 1)}

    def add(*args, **options):
        return fluxes(me, dense, weights, *args, count, **options)

    def keys(side):
        return tuple((p, side) for p in range(depth))

    def inside(half, to):
        return tuple((p, "xyz", half, to) for p in range(top)) + ((top, "xy", half, to),)

    def outside(to):
        return tuple((p, "z", half, to) for half in (0, 1) for p in (top, -1))

    _, sums, near_ends = add(None, inside(0, (0, 1)), sources, {}, (), keys(0) + keys(1), edges=((0, 0), (top, 0)), busy=False)
    lowest, highest = edges(me, near_ends, sides[1], (0, top), count)
    above = from_behind(lowest, "slab", -1)
    below = from_behind(highest, "slab", 1)
    for half in (0, 1):
        sources[depth, half] = ([above], 0)
        sources[-1, half] = ([below], 0)
    _, far_sums, _ = add(None, inside(1, (1,)), sources, {key: sums[key] for key in keys(1)}, (), keys(1))
    far_pieces, _, _ = add(weights_behind, outside((1,)), sources, far_sums, keys(1), ())
    near_sums = {key: sums[key] for key in keys(0)}
    near_pieces, _, _ = add(weights_behind, inside(1, (0,)) + outside((0,)), sources, near_sums, keys(0), ())
    back = exchange(list(near_pieces) + list(far_pieces), far + near)
    return unpack(me, (back,), (tuple(range(depth)),), field.shape)


def solution(mesh):
    in_specs = (P("mode", "slab", None, None), P(None, "slab", "mode", None), P(), P())
    out_specs = P("mode", "slab", None, None)
    return jax.shard_map(body, mesh=mesh, in_specs=in_specs, out_specs=out_specs, check_vma=False)
```

```python
import functools

import jax
import jax.numpy as jnp
from jax import lax
from jax.experimental import pallas as pl
from jax.experimental.pallas import tpu as pltpu
from jax.sharding import PartitionSpec as P

F32 = jnp.float32
BF16 = jnp.bfloat16
VMEM = pl.BlockSpec(memory_space=pltpu.VMEM)
SMEM = pl.BlockSpec(memory_space=pltpu.SMEM)
MIB = 2**20


def params(mib):
    return pltpu.CompilerParams(vmem_limit_bytes=mib * MIB)


def cost(flops, size):
    return pl.CostEstimate(flops=int(flops), bytes_accessed=int(size), transcendentals=0)


def from_behind(value, axis, steps):
    count = lax.axis_size(axis)
    first, last = (max(0, -steps), min(count, count - steps))
    return lax.ppermute(value, axis, [(source, source + steps) for source in range(first, last)])


def exchange(pieces, order):
    count = len(pieces)
    received = list(pieces)
    for s in order:
        received[s] = lax.ppermute(pieces[s], "mode", [(i, i ^ s) for i in range(count)])
    return received


def part_of(owner, size):
    return pl.ds(pl.multiple_of(owner * size, size), size)


def after(owner, count):
    return jnp.minimum(owner + 1, count - 1)


def split(value):
    high = value.astype(BF16)
    return high, (value - high.astype(F32)).astype(BF16)


def prepare_kernel(count, me_ref, pattern_ref, blocks_ref, field_ref, *outs):
    dense_refs, weights_ref = outs[:4], outs[4]
    fields, row_blocks, block, stored = blocks_ref.shape
    modes = row_blocks * block
    half = modes // 2
    lane = lax.broadcasted_iota(jnp.int32, (block, modes), 1)
    side = me_ref[0] // (count // 2)

    def one_field(k, carry):
        for j in range(row_blocks):
            rows_side, local = divmod(j, row_blocks // 2)
            r = (side ^ rows_side) * (row_blocks // 2) + local
            value = blocks_ref[k, r]
            value = jnp.concatenate([value, jnp.zeros((block, modes - stored), F32)], axis=1)
            total = None
            for c in range(stored // block):
                part = jnp.where((lane >= c * block) & (lane < (c + 1) * block), value, 0.0)
                shift = lax.rem(pattern_ref[k, r, c] - c + row_blocks, row_blocks) * block
                part = pltpu.roll(part, shift, 1)
                total = part if total is None else total + part
            total = pltpu.roll(total, side * half, 1)
            high, low = (part.astype(F32) for part in split(total))
            other_high, other_low = pltpu.roll(high, half, 1), pltpu.roll(low, half, 1)
            rows = pl.ds(pl.multiple_of(k * half + local * block, block), block)
            near = jnp.where(lane < half, high, other_low).astype(BF16), high[:, :half].astype(BF16)
            far = jnp.where(lane < half, other_high, low).astype(BF16), other_high[:, :half].astype(BF16)
            for columns_side, parts in enumerate((near, far)):
                dense_refs[2 * columns_side + rows_side][rows, 0:modes] = parts[0]
                dense_refs[2 * columns_side + rows_side][rows, modes:] = parts[1]
        return carry

    lax.fori_loop(0, fields, one_field, 0)
    for z in range(weights_ref.shape[0]):
        weights_ref[z] = jnp.swapaxes(field_ref[:, z], 0, 1)


def prepare(me, triple_blocks, block_pattern, coefficient_fields, count):
    fields, row_blocks, block, _ = triple_blocks.shape
    modes = row_blocks * block
    _, depth, rows, width = coefficient_fields.shape
    part = jax.ShapeDtypeStruct((fields * modes // 2, 3 * modes // 2), BF16)
    *parts, weights = pl.pallas_call(
        functools.partial(prepare_kernel, count),
        in_specs=[SMEM, SMEM, VMEM, VMEM],
        out_specs=[VMEM] * 5,
        out_shape=[part] * 4 + [jax.ShapeDtypeStruct((depth, rows, fields, width), F32)],
        compiler_params=params(16),
        cost_estimate=cost(1, 1),
        name="prepare",
    )(me, block_pattern, triple_blocks, coefficient_fields)
    return {(i // 2, i % 2): part for i, part in enumerate(parts)}, weights


def pack_kernel(count, me_ref, field_ref, *outs):
    me = me_ref[0]
    rows = field_ref.shape[2] // count
    for s, out in enumerate(outs):
        owner = me ^ s
        own = field_ref[:, 0, part_of(owner, rows), :]
        out[0, :rows] = jnp.swapaxes(own, 0, 1)
        ahead = field_ref[:, 0, part_of(after(owner, count), rows), :][:, 0]
        out[0, rows] = jnp.where(owner < count - 1, ahead, 0.0)


def pack(me, field, count):
    modes, depth, height, width = field.shape
    rows = height // count
    block = (1, rows + 1, modes, width)
    return pl.pallas_call(
        functools.partial(pack_kernel, count),
        grid=(depth,),
        in_specs=[SMEM, pl.BlockSpec((modes, 1, height, width), lambda i: (0, i, 0, 0))],
        out_specs=[pl.BlockSpec(block, lambda i: (i, 0, 0, 0))] * count,
        out_shape=[jax.ShapeDtypeStruct((depth,) + block[1:], F32)] * count,
        compiler_params=params(16),
        cost_estimate=cost(1, 1),
        name="pack",
    )(me, field)


def half_row(me, s, count, size):
    return part_of((me ^ s) & (count // 2 - 1), size)


def ahead_x(value):
    width = value.shape[-1]
    lane = lax.broadcasted_iota(jnp.int32, value.shape, 1)
    return jnp.where(lane == width - 1, 0.0, pltpu.roll(value, width - 1, 1))


def behind_x(value):
    lane = lax.broadcasted_iota(jnp.int32, value.shape, 1)
    return jnp.where(lane == 0, 0.0, pltpu.roll(value, 1, 1))


def edges_kernel(count, picks, me_ref, *refs):
    me = me_ref[0]
    near, far, outs = refs[: len(picks)], refs[len(picks) : len(picks) + count // 2], refs[len(picks) + count // 2 :]
    for out, own, index in zip(outs, near, picks):
        rows, modes, _ = out.shape
        out[:, : modes // 2, :] = own[...]
        for i, ref in enumerate(far):
            size = ref.shape[2]
            start = modes // 2 + ((me ^ (i + count // 2)) & (count // 2 - 1)) * size
            out[:, pl.ds(pl.multiple_of(start, size), size), :] = ref[index, :rows]


def edges(me, near, far, picks, count):
    rows, half, width = near[0].shape
    return pl.pallas_call(
        functools.partial(edges_kernel, count, picks),
        in_specs=[SMEM] + [VMEM] * (len(near) + len(far)),
        out_specs=[VMEM] * len(picks),
        out_shape=[jax.ShapeDtypeStruct((rows, 2 * half, width), F32)] * len(picks),
        compiler_params=params(16),
        cost_estimate=cost(1, 1),
        name="edges",
    )(me, *near, *far)


def couple(c_refs, rhs_ref, groups, weights, per_step):
    flat = [gradient for group in groups for gradient in group]
    owner = [r for r, group in enumerate(groups) for _ in group]
    half, width = flat[0].shape
    for i, gradient in enumerate(flat):
        high, low = split(gradient)
        lanes = slice(i * width, (i + 1) * width)
        rhs_ref[0:half, lanes] = high
        rhs_ref[half : 2 * half, lanes] = high
        rhs_ref[2 * half :, lanes] = low
    rhs = rhs_ref[:, : len(flat) * width]
    results = []
    for c_ref in c_refs:
        fields = c_ref.shape[0] // half
        totals = [None] * len(flat)
        for k0 in range(0, fields, per_step):
            product = jnp.dot(c_ref[k0 * half : (k0 + per_step) * half, :], rhs, preferred_element_type=F32)
            for k in range(per_step):
                for i in range(len(flat)):
                    part = product[k * half : (k + 1) * half, i * width : (i + 1) * width]
                    part = part * weights[owner[i]][k0 + k : k0 + k + 1, :]
                    totals[i] = part if totals[i] is None else totals[i] + part
        results.append(totals)
    return results


def flux_kernel(count, plan, me_ref, w_ref, *refs):
    tasks, dense_keys, sources, behind, sums_in, final, carried, edges = plan
    me = me_ref[0]
    refs = list(refs)
    dense = {key: refs.pop(0) for key in dense_keys}
    w_behind = refs.pop(0) if behind else None
    ins = [[refs.pop(0) for _ in range(number)] for _, _, number, _ in sources]
    sums = {key: refs.pop(0) for key in sums_in}
    outs = [refs.pop(0) for _ in range(count // 2 if final else 0)]
    total = {key: refs.pop(0) for key in carried}
    edge_refs = [refs.pop(0) for _ in edges]
    planes_ref, rhs_ref = refs.pop(0), refs.pop(0)
    for key in final:
        total[key] = refs.pop(0)
    _, full_rows, half_modes, width = planes_ref.shape
    rows = full_rows - 1
    slot = {}
    for (plane, half, _, index), group in zip(sources, ins):
        here = slot[plane, half] = len(slot)
        if len(group) == 1:
            planes_ref[here, :rows] = group[0][:, half * half_modes : (half + 1) * half_modes, :]
        else:
            for i, ref in enumerate(group):
                planes_ref[here, :, half_row(me, i + half * count // 2, count, ref.shape[2]), :] = ref[index]
    for ref, key in zip(edge_refs, edges):
        ref[...] = planes_ref[slot[key], :rows]
    for key, ref in total.items():
        ref[...] = sums[key][...] if key in sums else jnp.zeros_like(ref)

    for plane, directions, half, sides in tasks:
        per_step = 4 if len(directions) > 1 and len(dense_keys) > 1 else rows

        def step(i, carry, plane=plane, directions=directions, half=half, sides=sides, per_step=per_step):
            groups, weights = [], []
            for j in range(per_step):
                y = per_step * i + j
                here = planes_ref[slot[plane, half], y]
                group = []
                if "x" in directions:
                    group.append(ahead_x(here) - here)
                if "y" in directions:
                    group.append(planes_ref[slot[plane, half], y + 1] - here)
                if "z" in directions:
                    group.append(planes_ref[slot[plane + 1, half], y] - here)
                groups.append(group)
                weights.append(w_behind[0, y] if plane < 0 else w_ref[plane, y])
            results = couple([dense[half, side] for side in sides], rhs_ref, groups, weights, 4)
            for side, fluxes in zip(sides, results):
                here = total.get((plane, side))
                above = total.get((plane + 1, side))
                for j in range(per_step):
                    y = per_step * i + j
                    change = None
                    for direction in directions:
                        flux = fluxes.pop(0)
                        part = behind_x(flux) - flux if direction == "x" else -flux
                        change = part if change is None else change + part
                        if direction == "y":
                            here[y + 1] += flux
                        if direction == "z" and above is not None:
                            above[y] += flux
                    if here is not None:
                        here[y] += change
            return carry

        lax.fori_loop(0, rows // per_step, step, 0)
    side = final[0][1] if final else 0
    for i, out in enumerate(outs):
        for z, key in enumerate(final):
            out[z] = total[key][:, half_row(me, i + side * count // 2, count, out.shape[2]), :]


def fluxes(me, dense, weights, behind, tasks, sources, sums, final, carried, count, edges=(), busy=True):
    _, rows, fields, width = weights.shape
    half_modes = dense[0, 0].shape[0] // fields
    dense_keys = tuple(sorted({(half, side) for _, _, half, sides in tasks for side in sides}))
    needed = {(p, h) for p, _, h, _ in tasks} | {(p + 1, h) for p, directions, h, _ in tasks if "z" in directions}
    needed = sorted(needed | set(edges))
    listed = tuple((p, h, len(sources[p, h][0]), sources[p, h][1]) for p, h in needed)
    plan = (tasks, dense_keys, listed, behind is not None, tuple(sums), final, carried, edges)
    args = [weights] + [dense[key] for key in dense_keys] + ([] if behind is None else [behind])
    args += [array for key in needed for array in sources[key][0]] + list(sums.values())
    whole = (rows + 1, half_modes, width)
    piece = jax.ShapeDtypeStruct((len(final), rows + 1, 2 * half_modes // count, width), F32)
    out_shape = [piece] * (count // 2 if final else 0)
    number_out = len(out_shape)
    out_shape += [jax.ShapeDtypeStruct(whole, F32)] * len(carried)
    out_shape += [jax.ShapeDtypeStruct((rows, half_modes, width), F32)] * len(edges)
    scratch = [pltpu.VMEM((len(listed),) + whole, F32), pltpu.VMEM((3 * half_modes, (12 if len(dense_keys) > 1 else 3 * rows) * width), BF16)]
    scratch += [pltpu.VMEM(whole, F32)] * len(final)
    units = rows * sum(len(directions) * len(sides) for _, directions, _, sides in tasks)
    results = pl.pallas_call(
        functools.partial(flux_kernel, count, plan),
        in_specs=[SMEM] + [VMEM] * len(args),
        out_specs=[VMEM] * len(out_shape),
        out_shape=out_shape,
        scratch_shapes=scratch,
        compiler_params=params(32),
        cost_estimate=cost(busy * units * 4 * dense[0, 0].shape[0] * 2 * half_modes * width, 1),
        name="fluxes_" + "_".join(f"{p}{directions}{half}" for p, directions, half, _ in tasks),
    )(me, *args)
    sums_out = dict(zip(carried, results[number_out:]))
    return results[:number_out], sums_out, results[number_out + len(carried) :]


def unpack_kernel(count, chunks, me_ref, *refs):
    me = me_ref[0]
    step = pl.program_id(0)
    out = refs[-1]
    for c, planes in enumerate(chunks):
        chosen = functools.reduce(lambda left, right: left | right, [step == plane for plane in planes])

        @pl.when(chosen)
        def _(ins=refs[c * count : (c + 1) * count][::-1]):
            rows = ins[0].shape[1] - 1
            for s, ref in enumerate(ins):
                out[:, 0, part_of(me ^ s, rows), :] = jnp.swapaxes(ref[0, :rows], 0, 1)
            for s, ref in enumerate(ins):
                owner = me ^ s
                there = part_of(after(owner, count), rows)
                added = jnp.where(owner < count - 1, ref[0, rows], 0.0)[:, None, :]
                value = out[:, 0, there, :]
                row = lax.broadcasted_iota(jnp.int32, value.shape, 1)
                out[:, 0, there, :] = value + jnp.where(row == 0, added, 0.0)


def unpack(me, received, chunks, shape):
    modes, depth, height, width = shape
    count = len(received[0])
    in_specs, args = [SMEM], [me]
    for planes, pieces in zip(chunks, received):

        def place(i, planes=planes):
            return (functools.reduce(jnp.add, [(i >= plane).astype(jnp.int32) for plane in planes[1:]], 0), 0, 0, 0)

        in_specs += [pl.BlockSpec((1,) + pieces[0].shape[1:], place)] * count
        args += list(pieces)[::-1]
    return pl.pallas_call(
        functools.partial(unpack_kernel, count, chunks),
        grid=(depth,),
        in_specs=in_specs,
        out_specs=pl.BlockSpec((modes, 1, height, width), lambda i: (0, i, 0, 0)),
        out_shape=jax.ShapeDtypeStruct(shape, F32),
        compiler_params=params(16),
        cost_estimate=cost(1, 1),
        name="unpack",
    )(*args)


def body(field, coefficient_fields, triple_blocks, block_pattern):
    count = lax.axis_size("mode")
    depth = field.shape[1]
    top = depth - 1
    me = lax.axis_index("mode").astype(jnp.int32).reshape(1)
    near, far = tuple(range(1, count // 2)), tuple(range(count // 2, count))
    forth = far[:1] + near + far[1:]

    sent = exchange(pack(me, field, count), forth)
    dense, weights = prepare(me, triple_blocks, block_pattern, coefficient_fields, count)
    weights_behind = from_behind(weights[top:], "slab", 1)
    sides = (sent[: count // 2], sent[count // 2 :])
    sources = {(p, h): (sides[h], p) for p in range(depth) for h in (0, 1)}

    def add(*args, **options):
        return fluxes(me, dense, weights, *args, count, **options)

    def keys(side):
        return tuple((p, side) for p in range(depth))

    def inside(half, to):
        return tuple((p, "xyz", half, to) for p in range(top)) + ((top, "xy", half, to),)

    def outside(to):
        return tuple((p, "z", half, to) for half in (0, 1) for p in (top, -1))

    _, sums, near_ends = add(None, inside(0, (0, 1)), sources, {}, (), keys(0) + keys(1), edges=((0, 0), (top, 0)), busy=False)
    lowest, highest = edges(me, near_ends, sides[1], (0, top), count)
    above = from_behind(lowest, "slab", -1)
    below = from_behind(highest, "slab", 1)
    for half in (0, 1):
        sources[depth, half] = ([above], 0)
        sources[-1, half] = ([below], 0)
    _, far_sums, _ = add(None, inside(1, (1,)), sources, {key: sums[key] for key in keys(1)}, (), keys(1))
    far_pieces, _, _ = add(weights_behind, outside((1,)), sources, far_sums, keys(1), ())
    near_sums = {key: sums[key] for key in keys(0)}
    near_pieces, _, _ = add(weights_behind, inside(1, (0,)) + outside((0,)), sources, near_sums, keys(0), ())
    back = exchange(list(near_pieces) + list(far_pieces), far + near)
    return unpack(me, (back,), (tuple(range(depth)),), field.shape)


def solution(mesh):
    in_specs = (P("mode", "slab", None, None), P(None, "slab", "mode", None), P(), P())
    out_specs = P("mode", "slab", None, None)
    return jax.shard_map(body, mesh=mesh, in_specs=in_specs, out_specs=out_specs, check_vma=False)
```
